32 devices in a mesh: qrow: 8 (over y, x, core), dbcol: 4 (over z).
Axes of the slice: x: 2, y: 2, z: 4, core: 2. Of those that a mesh axis runs over, the one named last changes fastest.
Arguments:
- query_desc: bfloat16 [4096, 1024], P('qrow', 'dbcol'), may hold values from -0.1875 to 0.1875
- base_desc: bfloat16 [1024, 1024], P('dbcol', 'qrow'), may hold values from -6 to 6
- slopes: int32 [5], replicated, may hold values from -3 to 3, as said below
Outputs:
- seq_score: bfloat16 [4096, 1024], P('qrow', 'dbcol')
- best_score: float32 [4096], P('qrow')
The draws below stay inside these ranges and needn't reach their ends.
Inputs may be any that keep to these rules, and one draw needn't show every extreme that they name: `slopes`: 5 distinct values that always include -3 and 3.
All inputs are finite; a program needn't handle non-finite values.
Results may differ from the reference program's by a relative error of at most 0.0041.
Values may be sent and summed in bfloat16 or wider, within the bound.
A program may use at most 64 MiB of HBM per device.

```python
import math
import jax
import jax.numpy as jnp
from jax import lax

F = 1024
SEQ = 20
WIN = 10
SMAX = 3
NSLOPE = 5
ROWS_UP = 19
REACH = 57
HALO = 62
NQ = 4096
NB = 1024


def draw_slopes(key, part):
    middle = jax.random.permutation(key, jnp.arange(-SMAX + 1, SMAX, dtype=jnp.int32))[:NSLOPE - 2]
    return jnp.concatenate([jnp.array([-SMAX], jnp.int32), middle, jnp.array([SMAX], jnp.int32)])


def block_levels(rng, dims, cuts, smallest, largest):
    level, own = 1.0, jax.random.fold_in(rng, 6)
    for position, shards_of in cuts:
        steps = jnp.exp(jax.random.uniform(jax.random.fold_in(own, position), (shards_of,), jnp.float32, smallest / len(cuts), largest / len(cuts)))
        level = level * jnp.repeat(steps, dims[position] // shards_of).reshape([-1 if axis == position else 1 for axis in range(len(dims))])
    return level


def normal_values(stream_key, extent, scale, bound, split=(), kind=jnp.bfloat16):
    level = block_levels(stream_key, extent, split, -0.22, 0.18) if split else 1.0
    entries = jax.random.normal(stream_key, extent, jnp.float32) * scale * level
    return jnp.minimum(jnp.maximum(entries, -bound), bound).astype(kind)


def setup_inputs(seed: int = 0) -> dict:
    splits = jax.random.split(jax.random.key(seed), 4)
    query_desc = normal_values(splits[0], (NQ, F), F ** -0.5, 0.1875, ((0, 8), (1, 4)))
    base_desc = normal_values(splits[1], (NB, F), 1.0, 6.0, ((0, 4), (1, 8)))
    slopes = draw_slopes(jax.random.fold_in(splits[3], 71), 0)
    return {"query_desc": query_desc, "base_desc": base_desc, "slopes": slopes}


spread_floor = 0.5

def normalize(similar, valid_cols, valid_rows, out_cols):
    half_win = WIN // 2
    weights = valid_cols.astype(jnp.float32)
    masked = similar * weights[None, :]
    window_sum = masked[:, 0:out_cols]
    window_sq = window_sum * window_sum
    counts = weights[0:out_cols]
    for offset in range(1, WIN):
        column = masked[:, offset:offset + out_cols]
        window_sum = window_sum + column
        window_sq = window_sq + column * column
        counts = counts + weights[offset:offset + out_cols]
    counts = jnp.maximum(counts, 1.0)[None, :]
    window_mean = window_sum / counts
    window_var = window_sq / counts - window_mean * window_mean
    spread = jnp.sqrt(jnp.maximum(window_var, 0.0))
    middle = similar[:, half_win:half_win + out_cols]
    normed = (middle - window_mean) / jnp.maximum(spread, spread_floor)
    keep = weights[half_win:half_win + out_cols][None, :] * valid_rows.astype(jnp.float32)[:, None]
    return (normed * keep).astype(jnp.bfloat16)

def sequence_scores(normed, slopes, tile_rows, tile_cols):
    best_sum = None
    for slope_pos in range(NSLOPE):
        slope_now = slopes[slope_pos]
        running = jnp.zeros((tile_rows, tile_cols), jnp.float32)
        for back_step in range(SEQ):
            row_first = jnp.int32(ROWS_UP - back_step)
            col_first = (REACH - slope_now * back_step).astype(jnp.int32)
            window = lax.dynamic_slice(normed, (row_first, col_first), (tile_rows, tile_cols))
            running = running + window.astype(jnp.float32)
        best_sum = running if best_sum is None else jnp.maximum(best_sum, running)
    return best_sum * (1.0 / math.sqrt(SEQ))

def reference(query_desc, base_desc, slopes):
    block_rows = math.gcd(NQ, 512)
    query_padded = jnp.concatenate([jnp.zeros((ROWS_UP, F), jnp.bfloat16), query_desc], 0)
    base_padded = jnp.pad(base_desc, ((HALO, HALO), (0, 0)))
    column_ids = jnp.arange(NB + 2 * HALO, dtype=jnp.int32) - HALO
    valid_cols = (column_ids >= 0) & (column_ids < NB)

    def score_block(block_id):
        first_row = (block_id * block_rows).astype(jnp.int32)
        query_block = lax.dynamic_slice_in_dim(query_padded, first_row, block_rows + ROWS_UP, 0)
        similar = lax.dot_general(query_block, base_padded, (((1,), (1,)), ((), ())), preferred_element_type=jnp.float32)
        row_ids = first_row + jnp.arange(block_rows + ROWS_UP, dtype=jnp.int32) - ROWS_UP
        normed = normalize(similar, valid_cols, row_ids >= 0, NB + 2 * REACH)
        scores = sequence_scores(normed, slopes, block_rows, NB)
        return (scores.astype(jnp.bfloat16), lax.optimization_barrier(jnp.max(scores, axis=1)))
    seq_parts, best_parts = lax.map(score_block, jnp.arange(NQ // block_rows, dtype=jnp.int32))
    return (seq_parts.reshape(NQ, NB), best_parts.reshape(NQ))
```

```python
import functools
import math

import jax
import jax.numpy as jnp
from jax import lax
from jax.experimental import pallas as pl
from jax.experimental.pallas import tpu as pltpu
from jax.sharding import PartitionSpec as P

SEQ = 20
WIN = 10
SMAX = 3
NSLOPE = 5

SPREAD_FLOOR = 0.5
SIDE = 64
ABOVE = 24
EARLY = 32
STEP = 128
SUB, LANE = 8, 128
MESH = pl.DeviceIdType.MESH


def rolled(x, by):
    by %= x.shape[1]
    return pltpu.roll(x, by, 1) if by else x


def sheared(x, by, slope):
    if not slope:
        return rolled(x, by)
    width, tiles = x.shape[1], []
    for r in range(0, x.shape[0], SUB):
        tile, shift = x[r : r + SUB, :], (by + slope * r) % width
        if shift % LANE + slope * (SUB - 1) <= LANE:
            tile = pltpu.roll(tile, shift, 1, stride=slope, stride_axis=0)
        else:
            tile = rolled(pltpu.roll(tile, 0, 1, stride=slope, stride_axis=0), shift)
        tiles.append(tile)
    return jnp.concatenate(tiles, 0)


def window_sum(x):
    two = x + rolled(x, -1)
    four = two + rolled(two, -2)
    eight = four + rolled(four, -4)
    return rolled(eight + rolled(two, -8), WIN // 2)


def kernel(
    nq, nz, q_ref, b_ref, slopes_ref, seq_ref, best_ref, qs, bs, normed, tops,
    own_sem, side_send, side_recv, base_send, base_recv, ring_send, ring_recv,
    query_send, query_recv, up_send, up_recv, top_send, top_recv,
):
    me_q, me_z = lax.axis_index("qrow"), lax.axis_index("dbcol")
    rows, depth = q_ref.shape
    cols, base_depth = b_ref.shape
    width = cols + 2 * SIDE
    total = cols * nz
    first, last = me_z == 0, me_z == nz - 1

    def remote(src, dst, send, recv, q, z):
        return pltpu.make_async_remote_copy(
            src_ref=src, dst_ref=dst, send_sem=send, recv_sem=recv,
            device_id=(q, z), device_id_type=MESH,
        )

    slot_depth = bs.shape[2]

    def mine(start, count):
        if slot_depth == base_depth:
            return me_q, pl.ds(start, count), pl.ds(0, base_depth)
        return 0, pl.ds(start, count), pl.ds(pl.multiple_of(me_q * base_depth, LANE), base_depth)

    own = [
        pltpu.make_async_copy(q_ref, qs.at[me_z], own_sem.at[0]),
        pltpu.make_async_copy(b_ref, bs.at[mine(0, cols)], own_sem.at[1]),
    ]
    for copy in own:
        copy.start()

    q_peers = [lax.rem(me_q + d, nq) for d in range(1, nq)]
    z_peers = [lax.rem(me_z + d, nz) for d in range(1, nz)]
    barrier = pltpu.get_barrier_semaphore()
    for z in z_peers:
        pl.semaphore_signal(barrier, inc=1, device_id=(me_q, z), device_id_type=MESH)
    for q in q_peers:
        pl.semaphore_signal(barrier, inc=1, device_id=(q, me_z), device_id_type=MESH)

    @pl.when(last)
    def _():
        bs[mine(cols, SIDE)] = jnp.zeros((SIDE, base_depth), bs.dtype)

    @pl.when(first)
    def _():
        bs[mine(cols + SIDE, SIDE)] = jnp.zeros((SIDE, base_depth), bs.dtype)

    @pl.when(me_q == 0)
    def _():
        normed[0:ABOVE, :] = jnp.zeros((ABOVE, width), normed.dtype)

    pl.semaphore_wait(barrier, nq + nz - 2)

    to_left = remote(
        b_ref.at[pl.ds(0, SIDE), :], bs.at[mine(cols, SIDE)],
        side_send.at[0], side_recv.at[0], me_q, lax.max(me_z - 1, 0),
    )
    to_right = remote(
        b_ref.at[pl.ds(cols - SIDE, SIDE), :], bs.at[mine(cols + SIDE, SIDE)],
        side_send.at[1], side_recv.at[1], me_q, lax.min(me_z + 1, nz - 1),
    )

    @pl.when(jnp.logical_not(first))
    def _():
        to_left.start()

    @pl.when(jnp.logical_not(last))
    def _():
        to_right.start()

    pieces = [(rows - EARLY, EARLY)]
    pieces += [(r, min(STEP, rows - EARLY - r)) for r in range(0, rows, STEP)]

    def send_query(p):
        start, count = pieces[p]
        copies = [
            remote(
                q_ref.at[pl.ds(start, count), :], qs.at[me_z, pl.ds(start, count), :],
                query_send.at[p, d], query_recv.at[p, d], me_q, z,
            )
            for d, z in enumerate(z_peers)
        ]
        for copy in copies:
            copy.start()
        return copies

    query = [send_query(0)]
    base = [
        remote(b_ref, bs.at[mine(0, cols)], base_send.at[d], base_recv.at[d], q, me_z)
        for d, q in enumerate(q_peers)
    ]
    for copy in base:
        copy.start()
    for p in range(1, len(pieces)):
        query.append(send_query(p))

    @pl.when(jnp.logical_not(last))
    def _():
        to_left.wait_recv()

    @pl.when(jnp.logical_not(first))
    def _():
        to_right.wait_recv()

    sides = bs.at[mine(cols, 2 * SIDE)]
    ring = [
        remote(sides, sides, ring_send.at[d], ring_recv.at[d], q, me_z)
        for d, q in enumerate(q_peers)
    ]
    for copy in ring:
        copy.start()
    for copy in own:
        copy.wait()
    for copy in base + ring:
        copy.wait_recv()

    place = lax.broadcasted_iota(jnp.int32, (1, width), 1)
    frame = me_z * cols + jnp.where(place < cols + SIDE, place, place - width)
    inside = (frame >= 0) & (frame < total)
    reach = jnp.minimum(frame + WIN // 2, total) - jnp.maximum(frame - WIN // 2, 0)
    share = 1.0 / jnp.maximum(reach, 1).astype(jnp.float32)

    def normalize(start, count):
        similar = None
        deep = min(depth, slot_depth)
        for f in range(0, depth * nz, deep):
            part = lax.dot_general(
                qs[f // depth, start : start + count, f % depth : f % depth + deep],
                bs[f // slot_depth, :, f % slot_depth : f % slot_depth + deep],
                (((1,), (1,)), ((), ())), preferred_element_type=jnp.float32,
            )
            similar = part if similar is None else similar + part
        mean = window_sum(similar) * share
        var = window_sum(similar * similar) * share - mean * mean
        value = (similar - mean) * lax.rsqrt(jnp.maximum(var, SPREAD_FLOOR * SPREAD_FLOOR))
        value = jnp.where(inside, value, 0.0)
        normed[ABOVE + start : ABOVE + start + count, :] = value.astype(jnp.bfloat16).astype(
            jnp.float32
        )

    tried = {}
    for v in range(-SMAX, SMAX + 1):
        used = slopes_ref[0] == v
        for a in range(1, NSLOPE):
            used = used | (slopes_ref[a] == v)
        tried[v] = jnp.where(used, 0.0, -jnp.inf)

    span = ABOVE + STEP
    out_row = lax.broadcasted_iota(jnp.int32, (STEP, span), 0) + ABOVE
    in_row = lax.broadcasted_iota(jnp.int32, (STEP, span), 1)

    def summing(out, into):
        return ((into <= out) & (into > out - SEQ)).astype(jnp.bfloat16)

    band = summing(out_row, in_row)
    band_turned_in = summing(out_row, span - 1 - in_row)
    band_turned_out = summing(span + ABOVE - 1 - out_row, in_row)

    def turning(n, kind):
        row = lax.broadcasted_iota(jnp.int32, (n, n), 0)
        return (row + lax.broadcasted_iota(jnp.int32, (n, n), 1) == n - 1).astype(kind)

    turn_in, turn_out = turning(span, jnp.bfloat16), turning(STEP, jnp.float32)

    def score(start):
        block = normed[start : start + span, :]
        exact = block.astype(jnp.bfloat16)
        best = jnp.dot(band, exact, preferred_element_type=jnp.float32)[:, :cols] + tried[0]
        turned = jnp.dot(turn_in, exact, preferred_element_type=jnp.float32)
        down = None
        for v in range(1, SMAX + 1):
            lined = sheared(turned, -v * (span - 1), v).astype(jnp.bfloat16)
            sums = jnp.dot(band_turned_in, lined, preferred_element_type=jnp.float32)
            sums = sheared(sums, v * ABOVE, v)[:, :cols]
            best = jnp.maximum(best, sums + tried[v])
            lined = sheared(block, 0, v).astype(jnp.bfloat16)
            sums = jnp.dot(band_turned_out, lined, preferred_element_type=jnp.float32)
            sums = sheared(sums, -v * (span - 1), v)[:, :cols]
            sums = sums if v == SMAX else sums + tried[-v]
            down = sums if down is None else jnp.maximum(down, sums)
        down = jnp.dot(
            turn_out, down, precision=lax.Precision.HIGHEST, preferred_element_type=jnp.float32
        )
        best = jnp.maximum(best, down)
        best = best * (1.0 / math.sqrt(SEQ))
        seq_ref[start : start + STEP, :] = best.astype(seq_ref.dtype)
        top = best[:, 0:128]
        for c in range(128, cols, 128):
            top = jnp.maximum(top, best[:, c : c + 128])
        n = start // STEP
        tops[0, n : n + 1, :] = jnp.max(top.T, axis=0, keepdims=True)

    for copy in query[0]:
        copy.wait_recv()
    normalize(*pieces[0])
    up = remote(
        normed.at[pl.ds(rows, ABOVE), :], normed.at[pl.ds(0, ABOVE), :],
        up_send, up_recv, lax.min(me_q + 1, nq - 1), me_z,
    )

    @pl.when(me_q < nq - 1)
    def _():
        up.start()

    for p in range(1, len(pieces)):
        for copy in query[p]:
            copy.wait_recv()
        normalize(*pieces[p])
        if p == 1:

            @pl.when(me_q > 0)
            def _():
                up.wait_recv()

        score(pieces[p][0])

    peaks = [
        remote(tops.at[0], tops.at[1 + d], top_send.at[d], top_recv.at[d], me_q, z)
        for d, z in enumerate(z_peers)
    ]
    for copy in peaks:
        copy.start()

    @pl.when(jnp.logical_not(first))
    def _():
        to_left.wait_send()

    @pl.when(jnp.logical_not(last))
    def _():
        to_right.wait_send()

    @pl.when(me_q < nq - 1)
    def _():
        up.wait_send()

    for copy in base + ring:
        copy.wait_send()
    for copies in query:
        for copy in copies:
            copy.wait_send()
    for copy in peaks:
        copy.wait()
    best = tops[0]
    for d in range(1, nz):
        best = jnp.maximum(best, tops[d])
    best_ref[...] = best


def solution(mesh):
    nq, nz = mesh.shape["qrow"], mesh.shape["dbcol"]

    def local(query_desc, base_desc, slopes):
        rows, depth = query_desc.shape
        cols, base_depth = base_desc.shape
        width = cols + 2 * SIDE
        slots = (nq, width, base_depth) if base_depth % LANE else (1, width, base_depth * nq)
        steps = rows // STEP
        dma = pltpu.SemaphoreType.DMA
        any_space = pl.BlockSpec(memory_space=pl.ANY)
        vmem = pl.BlockSpec(memory_space=pltpu.VMEM)
        seq_score, best = pl.pallas_call(
            functools.partial(kernel, nq, nz),
            out_shape=(
                jax.ShapeDtypeStruct((rows, cols), jnp.bfloat16),
                jax.ShapeDtypeStruct((steps, STEP), jnp.float32),
            ),
            in_specs=[any_space, any_space, pl.BlockSpec(memory_space=pltpu.SMEM)],
            out_specs=(vmem, vmem),
            scratch_shapes=[
                pltpu.VMEM((nz, rows, depth), jnp.bfloat16),
                pltpu.VMEM(slots, jnp.bfloat16),
                pltpu.VMEM((ABOVE + rows, width), jnp.float32),
                pltpu.VMEM((nz, steps, STEP), jnp.float32),
                dma((2,)),
                dma((2,)),
                dma((2,)),
                dma((nq - 1,)),
                dma((nq - 1,)),
                dma((nq - 1,)),
                dma((nq - 1,)),
                dma((steps + 1, nz - 1)),
                dma((steps + 1, nz - 1)),
                dma(()),
                dma(()),
                dma((nz - 1,)),
                dma((nz - 1,)),
            ],
            compiler_params=pltpu.CompilerParams(
                collective_id=0, has_side_effects=True, vmem_limit_bytes=40 << 20
            ),
            cost_estimate=pl.CostEstimate(
                flops=2 * rows * width * depth * nz,
                bytes_accessed=4 * rows * cols,
                transcendentals=rows * width,
            ),
        )(query_desc, base_desc, slopes)
        return seq_score, best.reshape(rows)

    return jax.shard_map(
        local,
        mesh=mesh,
        in_specs=(P("qrow", "dbcol"), P("dbcol", "qrow"), P()),
        out_specs=(P("qrow", "dbcol"), P("qrow")),
        check_vma=False,
    )
```

```python
import functools
import math

import jax
import jax.numpy as jnp
from jax import lax
from jax.experimental import pallas as pl
from jax.experimental.pallas import tpu as pltpu
from jax.sharding import PartitionSpec as P

SEQ = 20
WIN = 10
SMAX = 3
NSLOPE = 5

SPREAD_FLOOR = 0.5
SIDE = 64
ABOVE = 24
EARLY = 32
AHEAD = 3
STEP = 128
SUB, LANE = 8, 128
MESH = pl.DeviceIdType.MESH


def rolled(x, by):
    by %= x.shape[1]
    return pltpu.roll(x, by, 1) if by else x


def sheared(x, by, slope):
    if not slope:
        return rolled(x, by)
    width, tiles = x.shape[1], []
    for r in range(0, x.shape[0], SUB):
        tile, shift = x[r : r + SUB, :], (by + slope * r) % width
        if shift % LANE + slope * (SUB - 1) <= LANE:
            tile = pltpu.roll(tile, shift, 1, stride=slope, stride_axis=0)
        else:
            tile = rolled(pltpu.roll(tile, 0, 1, stride=slope, stride_axis=0), shift)
        tiles.append(tile)
    return jnp.concatenate(tiles, 0)


def window_sum(x):
    two = x + rolled(x, -1)
    four = two + rolled(two, -2)
    eight = four + rolled(four, -4)
    return rolled(eight + rolled(two, -8), WIN // 2)


def kernel(
    nq, nz, q_ref, b_ref, slopes_hbm, seq_hbm, best_ref, seq_ref, qs, bs, bt, normed, tops, slopes_ref,
    own_sem, out_sem, side_send, side_recv, base_send, base_recv, ring_send, ring_recv,
    query_send, query_recv, up_send, up_recv, top_send, top_recv,
):
    me_q, me_z = lax.axis_index("qrow"), lax.axis_index("dbcol")
    rows, depth = q_ref.shape
    cols, base_depth = b_ref.shape
    width = cols + 2 * SIDE
    total = cols * nz
    first, last = me_z == 0, me_z == nz - 1

    def remote(src, dst, send, recv, q, z):
        return pltpu.make_async_remote_copy(
            src_ref=src, dst_ref=dst, send_sem=send, recv_sem=recv,
            device_id=(q, z), device_id_type=MESH,
        )

    slot_depth = bs.shape[2]

    def mine(start, count):
        if slot_depth == base_depth:
            return me_q, pl.ds(start, count), pl.ds(0, base_depth)
        return 0, pl.ds(start, count), pl.ds(pl.multiple_of(me_q * base_depth, LANE), base_depth)

    own = [
        pltpu.make_async_copy(q_ref, qs.at[me_z], own_sem.at[0]),
        pltpu.make_async_copy(b_ref, bs.at[mine(0, cols)], own_sem.at[1]),
        pltpu.make_async_copy(slopes_hbm, slopes_ref, own_sem.at[2]),
    ]
    for copy in own:
        copy.start()

    q_peers = [lax.rem(me_q + d, nq) for d in range(1, nq)]
    z_peers = [lax.rem(me_z + d, nz) for d in range(1, nz)]
    barrier = pltpu.get_barrier_semaphore()
    for z in z_peers:
        pl.semaphore_signal(barrier, inc=1, device_id=(me_q, z), device_id_type=MESH)
    for q in q_peers:
        pl.semaphore_signal(barrier, inc=1, device_id=(q, me_z), device_id_type=MESH)

    @pl.when(last)
    def _():
        bs[mine(cols, SIDE)] = jnp.zeros((SIDE, base_depth), bs.dtype)

    @pl.when(first)
    def _():
        bs[mine(cols + SIDE, SIDE)] = jnp.zeros((SIDE, base_depth), bs.dtype)

    @pl.when(me_q == 0)
    def _():
        normed[0:ABOVE, :] = jnp.zeros((ABOVE, width), normed.dtype)

    pl.semaphore_wait(barrier, nq + nz - 2)

    to_left = remote(
        b_ref.at[pl.ds(0, SIDE), :], bs.at[mine(cols, SIDE)],
        side_send.at[0], side_recv.at[0], me_q, lax.max(me_z - 1, 0),
    )
    to_right = remote(
        b_ref.at[pl.ds(cols - SIDE, SIDE), :], bs.at[mine(cols + SIDE, SIDE)],
        side_send.at[1], side_recv.at[1], me_q, lax.min(me_z + 1, nz - 1),
    )

    @pl.when(jnp.logical_not(first))
    def _():
        to_left.start()

    @pl.when(jnp.logical_not(last))
    def _():
        to_right.start()

    pieces = [(rows - EARLY, EARLY)]
    pieces += [(r, min(STEP, rows - EARLY - r)) for r in range(0, rows, STEP)]

    def send_query(p):
        start, count = pieces[p]
        copies = [
            remote(
                q_ref.at[pl.ds(start, count), :], qs.at[me_z, pl.ds(start, count), :],
                query_send.at[p, d], query_recv.at[p, d], me_q, z,
            )
            for d, z in enumerate(z_peers)
        ]
        for copy in copies:
            copy.start()
        return copies

    query = [send_query(0)]
    base = [
        remote(b_ref, bs.at[mine(0, cols)], base_send.at[d], base_recv.at[d], q, me_z)
        for d, q in enumerate(q_peers)
    ]
    for copy in base:
        copy.start()
    for p in range(1, AHEAD):
        query.append(send_query(p))

    @pl.when(jnp.logical_not(last))
    def _():
        to_left.wait_recv()

    @pl.when(jnp.logical_not(first))
    def _():
        to_right.wait_recv()

    sides = bs.at[mine(cols, 2 * SIDE)]
    ring = [
        remote(sides, sides, ring_send.at[d], ring_recv.at[d], q, me_z)
        for d, q in enumerate(q_peers)
    ]
    for copy in ring:
        copy.start()
    for copy in own:
        copy.wait()
    for d in range(nq):
        q = lax.rem(me_q + nq - d, nq)
        if d:
            base[d - 1].wait_recv()
            ring[d - 1].wait_recv()
        start = pl.multiple_of(q * base_depth, base_depth)
        if slot_depth == base_depth:
            part = bs[q, :, :]
        else:
            part = bs[0, :, pl.ds(start, base_depth)]
        bt[pl.ds(start, base_depth), :] = part.T

    place = lax.broadcasted_iota(jnp.int32, (1, width), 1)
    frame = me_z * cols + jnp.where(place < cols + SIDE, place, place - width)
    inside = (frame >= 0) & (frame < total)
    reach = jnp.minimum(frame + WIN // 2, total) - jnp.maximum(frame - WIN // 2, 0)
    share = 1.0 / jnp.maximum(reach, 1).astype(jnp.float32)

    def normalize(start, count):
        similar = None
        for z in range(nz):
            part = jnp.dot(
                qs[z, start : start + count, :], bt[z * depth : (z + 1) * depth, :],
                preferred_element_type=jnp.float32,
            )
            similar = part if similar is None else similar + part
        mean = window_sum(similar) * share
        var = window_sum(similar * similar) * share - mean * mean
        value = (similar - mean) * lax.rsqrt(jnp.maximum(var, SPREAD_FLOOR * SPREAD_FLOOR))
        value = jnp.where(inside, value, 0.0)
        normed[ABOVE + start : ABOVE + start + count, :] = value.astype(jnp.bfloat16).astype(
            jnp.float32
        )

    tried = {}
    for v in range(-SMAX, SMAX + 1):
        used = slopes_ref[0] == v
        for a in range(1, NSLOPE):
            used = used | (slopes_ref[a] == v)
        tried[v] = jnp.where(used, 0.0, -jnp.inf)

    span = ABOVE + STEP
    out_row = lax.broadcasted_iota(jnp.int32, (STEP, span), 0) + ABOVE
    in_row = lax.broadcasted_iota(jnp.int32, (STEP, span), 1)

    def summing(out, into):
        return ((into <= out) & (into > out - SEQ)).astype(jnp.bfloat16)

    band = summing(out_row, in_row)
    band_turned_in = summing(out_row, span - 1 - in_row)
    band_turned_out = summing(span + ABOVE - 1 - out_row, in_row)

    def turning(n, kind):
        row = lax.broadcasted_iota(jnp.int32, (n, n), 0)
        return (row + lax.broadcasted_iota(jnp.int32, (n, n), 1) == n - 1).astype(kind)

    turn_in, turn_out = turning(span, jnp.bfloat16), turning(STEP, jnp.float32)

    written = []

    def score(start):
        block = normed[start : start + span, :]
        exact = block.astype(jnp.bfloat16)
        best = jnp.dot(band, exact, preferred_element_type=jnp.float32)[:, :cols] + tried[0]
        turned = jnp.dot(turn_in, exact, preferred_element_type=jnp.float32)
        down = None
        for v in range(1, SMAX + 1):
            lined = sheared(turned, -v * (span - 1), v).astype(jnp.bfloat16)
            sums = jnp.dot(band_turned_in, lined, preferred_element_type=jnp.float32)
            sums = sheared(sums, v * ABOVE, v)[:, :cols]
            best = jnp.maximum(best, sums + tried[v])
            lined = sheared(block, 0, v).astype(jnp.bfloat16)
            sums = jnp.dot(band_turned_out, lined, preferred_element_type=jnp.float32)
            sums = sheared(sums, -v * (span - 1), v)[:, :cols]
            sums = sums if v == SMAX else sums + tried[-v]
            down = sums if down is None else jnp.maximum(down, sums)
        down = jnp.dot(
            turn_out, down, precision=lax.Precision.HIGHEST, preferred_element_type=jnp.float32
        )
        best = jnp.maximum(best, down)
        best = best * (1.0 / math.sqrt(SEQ))
        done = pl.ds(start, STEP)
        seq_ref[done, :] = best.astype(seq_ref.dtype)
        written.append(
            pltpu.make_async_copy(
                seq_ref.at[done, :], seq_hbm.at[done, :], out_sem.at[start // STEP]
            )
        )
        written[-1].start()
        top = best[:, 0:128]
        for c in range(128, cols, 128):
            top = jnp.maximum(top, best[:, c : c + 128])
        n = start // STEP
        tops[0, n : n + 1, :] = jnp.max(top.T, axis=0, keepdims=True)

    for copy in query[0]:
        copy.wait_recv()
    normalize(*pieces[0])
    up = remote(
        normed.at[pl.ds(rows, ABOVE), :], normed.at[pl.ds(0, ABOVE), :],
        up_send, up_recv, lax.min(me_q + 1, nq - 1), me_z,
    )

    @pl.when(me_q < nq - 1)
    def _():
        up.start()

    for p in range(1, len(pieces)):
        for copy in query[p]:
            copy.wait_recv()
        if p + AHEAD - 1 < len(pieces):
            for copy in query[p]:
                copy.wait_send()
            query.append(send_query(p + AHEAD - 1))
        normalize(*pieces[p])
        if p == 1:

            @pl.when(me_q > 0)
            def _():
                up.wait_recv()

        score(pieces[p][0])

    peaks = [
        remote(tops.at[0], tops.at[1 + d], top_send.at[d], top_recv.at[d], me_q, z)
        for d, z in enumerate(z_peers)
    ]
    for copy in peaks:
        copy.start()

    @pl.when(jnp.logical_not(first))
    def _():
        to_left.wait_send()

    @pl.when(jnp.logical_not(last))
    def _():
        to_right.wait_send()

    @pl.when(me_q < nq - 1)
    def _():
        up.wait_send()

    for copy in base + ring:
        copy.wait_send()
    for p in [0] + list(range(max(1, len(pieces) - AHEAD + 1), len(pieces))):
        for copy in query[p]:
            copy.wait_send()
    for copy in written + peaks:
        copy.wait()
    best = tops[0]
    for d in range(1, nz):
        best = jnp.maximum(best, tops[d])
    best_ref[...] = best


def solution(mesh):
    nq, nz = mesh.shape["qrow"], mesh.shape["dbcol"]

    def local(query_desc, base_desc, slopes):
        rows, depth = query_desc.shape
        cols, base_depth = base_desc.shape
        width = cols + 2 * SIDE
        slots = (nq, width, base_depth) if base_depth % LANE else (1, width, base_depth * nq)
        steps = rows // STEP
        dma = pltpu.SemaphoreType.DMA
        hbm = pl.BlockSpec(memory_space=pltpu.HBM)
        vmem = pl.BlockSpec(memory_space=pltpu.VMEM)
        seq_score, best = pl.pallas_call(
            functools.partial(kernel, nq, nz),
            out_shape=(
                jax.ShapeDtypeStruct((rows, cols), jnp.bfloat16),
                jax.ShapeDtypeStruct((steps, STEP), jnp.float32),
            ),
            in_specs=[hbm, hbm, hbm],
            out_specs=(hbm, vmem),
            scratch_shapes=[
                pltpu.VMEM((rows, cols), jnp.bfloat16),
                pltpu.VMEM((nz, rows, depth), jnp.bfloat16),
                pltpu.VMEM(slots, jnp.bfloat16),
                pltpu.VMEM((base_depth * nq, width), jnp.bfloat16),
                pltpu.VMEM((ABOVE + rows, width), jnp.float32),
                pltpu.VMEM((nz, steps, STEP), jnp.float32),
                pltpu.SMEM((NSLOPE,), jnp.int32),
                dma((3,)),
                dma((steps,)),
                dma((2,)),
                dma((2,)),
                dma((nq - 1,)),
                dma((nq - 1,)),
                dma((nq - 1,)),
                dma((nq - 1,)),
                dma((steps + 1, nz - 1)),
                dma((steps + 1, nz - 1)),
                dma(()),
                dma(()),
                dma((nz - 1,)),
                dma((nz - 1,)),
            ],
            compiler_params=pltpu.CompilerParams(
                collective_id=0, has_side_effects=True, vmem_limit_bytes=60 << 20
            ),
            cost_estimate=pl.CostEstimate(
                flops=2 * rows * width * depth * nz,
                bytes_accessed=4 * rows * cols,
                transcendentals=rows * width,
            ),
        )(query_desc, base_desc, slopes)
        return seq_score, best.reshape(rows)

    return jax.shard_map(
        local,
        mesh=mesh,
        in_specs=(P("qrow", "dbcol"), P("dbcol", "qrow"), P()),
        out_specs=(P("qrow", "dbcol"), P("qrow")),
        check_vma=False,
    )
```

```python
import functools
import math

import jax
import jax.numpy as jnp
from jax import lax
from jax.experimental import pallas as pl
from jax.experimental.pallas import tpu as pltpu
from jax.sharding import PartitionSpec as P

SEQ = 20
WIN = 10
SMAX = 3
NSLOPE = 5

SPREAD_FLOOR = 0.5
SIDE = 64
ABOVE = 24
EARLY = 32
AHEAD = 3
STEP = 128
SUB, LANE = 8, 128
MESH = pl.DeviceIdType.MESH


def rolled(x, by):
    by %= x.shape[1]
    return pltpu.roll(x, by, 1) if by else x


def sheared(x, by, slope):
    if not slope:
        return rolled(x, by)
    width, tiles = x.shape[1], []
    for r in range(0, x.shape[0], SUB):
        tile, shift = x[r : r + SUB, :], (by + slope * r) % width
        if shift % LANE + slope * (SUB - 1) <= LANE:
            tile = pltpu.roll(tile, shift, 1, stride=slope, stride_axis=0)
        else:
            tile = rolled(pltpu.roll(tile, 0, 1, stride=slope, stride_axis=0), shift)
        tiles.append(tile)
    return jnp.concatenate(tiles, 0)


def window_sum(x):
    two = x + rolled(x, -1)
    four = two + rolled(two, -2)
    eight = four + rolled(four, -4)
    return rolled(eight + rolled(two, -8), WIN // 2)


def kernel(
    nq, nz, q_ref, b_ref, slopes_hbm, seq_hbm, best_ref, seq_ref, qs, bs, bt, normed, tops, slopes_ref,
    own_sem, out_sem, side_send, side_recv, base_send, base_recv, pass_send, pass_recv,
    query_send, query_recv, up_send, up_recv, top_send, top_recv,
):
    me_q, me_z = lax.axis_index("qrow"), lax.axis_index("dbcol")
    rows, depth = q_ref.shape
    cols, base_depth = b_ref.shape
    width = cols + 2 * SIDE
    total = cols * nz
    first, last = me_z == 0, me_z == nz - 1

    def remote(src, dst, send, recv, q, z):
        return pltpu.make_async_remote_copy(
            src_ref=src, dst_ref=dst, send_sem=send, recv_sem=recv,
            device_id=(q, z), device_id_type=MESH,
        )

    slot_depth = bs.shape[2]

    def mine(start, count):
        if slot_depth == base_depth:
            return me_q, pl.ds(start, count), pl.ds(0, base_depth)
        return 0, pl.ds(start, count), pl.ds(pl.multiple_of(me_q * base_depth, LANE), base_depth)

    own = [
        pltpu.make_async_copy(q_ref, qs.at[me_z], own_sem.at[0]),
        pltpu.make_async_copy(b_ref, bs.at[mine(0, cols)], own_sem.at[1]),
        pltpu.make_async_copy(slopes_hbm, slopes_ref, own_sem.at[2]),
    ]
    for copy in own:
        copy.start()

    q_peers = [lax.rem(me_q + d, nq) for d in range(1, nq)]
    z_peers = [lax.rem(me_z + d, nz) for d in range(1, nz)]
    barrier = pltpu.get_barrier_semaphore()
    for z in z_peers:
        pl.semaphore_signal(barrier, inc=1, device_id=(me_q, z), device_id_type=MESH)
    for q in q_peers:
        pl.semaphore_signal(barrier, inc=1, device_id=(q, me_z), device_id_type=MESH)

    @pl.when(last)
    def _():
        bs[mine(cols, SIDE)] = jnp.zeros((SIDE, base_depth), bs.dtype)

    @pl.when(first)
    def _():
        bs[mine(cols + SIDE, SIDE)] = jnp.zeros((SIDE, base_depth), bs.dtype)

    @pl.when(me_q == 0)
    def _():
        normed[0:ABOVE, :] = jnp.zeros((ABOVE, width), normed.dtype)

    pl.semaphore_wait(barrier, nq + nz - 2)

    to_left = remote(
        b_ref.at[pl.ds(0, SIDE), :], bs.at[mine(cols, SIDE)],
        side_send.at[0], side_recv.at[0], me_q, lax.max(me_z - 1, 0),
    )
    to_right = remote(
        b_ref.at[pl.ds(cols - SIDE, SIDE), :], bs.at[mine(cols + SIDE, SIDE)],
        side_send.at[1], side_recv.at[1], me_q, lax.min(me_z + 1, nz - 1),
    )

    @pl.when(jnp.logical_not(first))
    def _():
        to_left.start()

    @pl.when(jnp.logical_not(last))
    def _():
        to_right.start()

    pieces = [(rows - EARLY, EARLY)]
    pieces += [(r, min(STEP, rows - EARLY - r)) for r in range(0, rows, STEP)]

    def send_query(p):
        start, count = pieces[p]
        copies = [
            remote(
                q_ref.at[pl.ds(start, count), :], qs.at[me_z, pl.ds(start, count), :],
                query_send.at[p, d], query_recv.at[p, d], me_q, z,
            )
            for d, z in enumerate(z_peers)
        ]
        for copy in copies:
            copy.start()
        return copies

    query = [send_query(p) for p in range(AHEAD - 1)]

    @pl.when(jnp.logical_not(last))
    def _():
        to_left.wait_recv()

    @pl.when(jnp.logical_not(first))
    def _():
        to_right.wait_recv()

    for copy in own:
        copy.wait()

    def block(q):
        if slot_depth == base_depth:
            return bs.at[q]
        start = pl.multiple_of(q * base_depth, LANE)
        return bs.at[0, :, pl.ds(start, base_depth)]

    def hand_on(q, d):
        copy = remote(block(q), block(q), pass_send.at[d], pass_recv.at[d], mate, me_z)
        copy.start()
        return copy

    def turn(q):
        start = pl.multiple_of(q * base_depth, base_depth)
        bt[pl.ds(start, base_depth), :] = block(q)[...].T

    mate = me_q + 1 - 2 * lax.rem(me_q, 2)
    base = [
        remote(
            block(me_q), block(me_q), base_send.at[d - 1], base_recv.at[d - 1],
            lax.rem(me_q + 2 * d, nq), me_z,
        )
        for d in range(1, nq // 2)
    ]
    for copy in base:
        copy.start()
    handed = [hand_on(me_q, 0)]
    query.append(send_query(AHEAD - 1))
    turn(me_q)
    for d in range(1, nq // 2):
        base[d - 1].wait_recv()
        q = lax.rem(me_q + nq - 2 * d, nq)
        handed.append(hand_on(q, d))
        turn(q)
    for d in range(nq // 2):
        handed[d].wait_recv()
        turn(lax.rem(mate + nq - 2 * d, nq))

    place = lax.broadcasted_iota(jnp.int32, (1, width), 1)
    frame = me_z * cols + jnp.where(place < cols + SIDE, place, place - width)
    inside = (frame >= 0) & (frame < total)
    reach = jnp.minimum(frame + WIN // 2, total) - jnp.maximum(frame - WIN // 2, 0)
    share = 1.0 / jnp.maximum(reach, 1).astype(jnp.float32)

    def normalize(start, count):
        similar = None
        for z in range(nz):
            part = jnp.dot(
                qs[z, start : start + count, :], bt[z * depth : (z + 1) * depth, :],
                preferred_element_type=jnp.float32,
            )
            similar = part if similar is None else similar + part
        mean = window_sum(similar) * share
        var = window_sum(similar * similar) * share - mean * mean
        value = (similar - mean) * lax.rsqrt(jnp.maximum(var, SPREAD_FLOOR * SPREAD_FLOOR))
        value = jnp.where(inside, value, 0.0)
        normed[ABOVE + start : ABOVE + start + count, :] = value.astype(jnp.bfloat16).astype(
            jnp.float32
        )

    tried = {}
    for v in range(-SMAX, SMAX + 1):
        used = slopes_ref[0] == v
        for a in range(1, NSLOPE):
            used = used | (slopes_ref[a] == v)
        tried[v] = jnp.where(used, 0.0, -jnp.inf)

    span = ABOVE + STEP
    out_row = lax.broadcasted_iota(jnp.int32, (STEP, span), 0) + ABOVE
    in_row = lax.broadcasted_iota(jnp.int32, (STEP, span), 1)

    def summing(out, into):
        return ((into <= out) & (into > out - SEQ)).astype(jnp.bfloat16)

    band = summing(out_row, in_row)
    band_turned_in = summing(out_row, span - 1 - in_row)
    band_turned_out = summing(span + ABOVE - 1 - out_row, in_row)

    def turning(n, kind):
        row = lax.broadcasted_iota(jnp.int32, (n, n), 0)
        return (row + lax.broadcasted_iota(jnp.int32, (n, n), 1) == n - 1).astype(kind)

    turn_in, turn_out = turning(span, jnp.bfloat16), turning(STEP, jnp.float32)

    written = []

    def score(start):
        block = normed[start : start + span, :]
        exact = block.astype(jnp.bfloat16)
        best = jnp.dot(band, exact, preferred_element_type=jnp.float32)[:, :cols] + tried[0]
        turned = jnp.dot(turn_in, exact, preferred_element_type=jnp.float32)
        down = None
        for v in range(1, SMAX + 1):
            lined = sheared(turned, -v * (span - 1), v).astype(jnp.bfloat16)
            sums = jnp.dot(band_turned_in, lined, preferred_element_type=jnp.float32)
            sums = sheared(sums, v * ABOVE, v)[:, :cols]
            best = jnp.maximum(best, sums + tried[v])
            lined = sheared(block, 0, v).astype(jnp.bfloat16)
            sums = jnp.dot(band_turned_out, lined, preferred_element_type=jnp.float32)
            sums = sheared(sums, -v * (span - 1), v)[:, :cols]
            sums = sums if v == SMAX else sums + tried[-v]
            down = sums if down is None else jnp.maximum(down, sums)
        down = jnp.dot(
            turn_out, down, precision=lax.Precision.HIGHEST, preferred_element_type=jnp.float32
        )
        best = jnp.maximum(best, down)
        best = best * (1.0 / math.sqrt(SEQ))
        done = pl.ds(start, STEP)
        seq_ref[done, :] = best.astype(seq_ref.dtype)
        written.append(
            pltpu.make_async_copy(
                seq_ref.at[done, :], seq_hbm.at[done, :], out_sem.at[start // STEP]
            )
        )
        written[-1].start()
        top = best[:, 0:128]
        for c in range(128, cols, 128):
            top = jnp.maximum(top, best[:, c : c + 128])
        n = start // STEP
        tops[0, n : n + 1, :] = jnp.max(top.T, axis=0, keepdims=True)

    for copy in query[0]:
        copy.wait_recv()
    normalize(*pieces[0])
    up = remote(
        normed.at[pl.ds(rows, ABOVE), :], normed.at[pl.ds(0, ABOVE), :],
        up_send, up_recv, lax.min(me_q + 1, nq - 1), me_z,
    )

    @pl.when(me_q < nq - 1)
    def _():
        up.start()

    for p in range(1, len(pieces)):
        for copy in query[p]:
            copy.wait_recv()
        if p + AHEAD - 1 < len(pieces):
            for copy in query[p]:
                copy.wait_send()
            query.append(send_query(p + AHEAD - 1))
        normalize(*pieces[p])
        if p == 1:

            @pl.when(me_q > 0)
            def _():
                up.wait_recv()

        score(pieces[p][0])

    peaks = [
        remote(tops.at[0], tops.at[1 + d], top_send.at[d], top_recv.at[d], me_q, z)
        for d, z in enumerate(z_peers)
    ]
    for copy in peaks:
        copy.start()

    @pl.when(jnp.logical_not(first))
    def _():
        to_left.wait_send()

    @pl.when(jnp.logical_not(last))
    def _():
        to_right.wait_send()

    @pl.when(me_q < nq - 1)
    def _():
        up.wait_send()

    for copy in base + handed:
        copy.wait_send()
    for p in [0] + list(range(max(1, len(pieces) - AHEAD + 1), len(pieces))):
        for copy in query[p]:
            copy.wait_send()
    for copy in written + peaks:
        copy.wait()
    best = tops[0]
    for d in range(1, nz):
        best = jnp.maximum(best, tops[d])
    best_ref[...] = best


def solution(mesh):
    nq, nz = mesh.shape["qrow"], mesh.shape["dbcol"]

    def local(query_desc, base_desc, slopes):
        rows, depth = query_desc.shape
        cols, base_depth = base_desc.shape
        width = cols + 2 * SIDE
        slots = (nq, width, base_depth) if base_depth % LANE else (1, width, base_depth * nq)
        steps = rows // STEP
        dma = pltpu.SemaphoreType.DMA
        hbm = pl.BlockSpec(memory_space=pltpu.HBM)
        vmem = pl.BlockSpec(memory_space=pltpu.VMEM)
        seq_score, best = pl.pallas_call(
            functools.partial(kernel, nq, nz),
            out_shape=(
                jax.ShapeDtypeStruct((rows, cols), jnp.bfloat16),
                jax.ShapeDtypeStruct((steps, STEP), jnp.float32),
            ),
            in_specs=[hbm, hbm, hbm],
            out_specs=(hbm, vmem),
            scratch_shapes=[
                pltpu.VMEM((rows, cols), jnp.bfloat16),
                pltpu.VMEM((nz, rows, depth), jnp.bfloat16),
                pltpu.VMEM(slots, jnp.bfloat16),
                pltpu.VMEM((base_depth * nq, width), jnp.bfloat16),
                pltpu.VMEM((ABOVE + rows, width), jnp.float32),
                pltpu.VMEM((nz, steps, STEP), jnp.float32),
                pltpu.SMEM((NSLOPE,), jnp.int32),
                dma((3,)),
                dma((steps,)),
                dma((2,)),
                dma((2,)),
                dma((nq // 2 - 1,)),
                dma((nq // 2 - 1,)),
                dma((nq // 2,)),
                dma((nq // 2,)),
                dma((steps + 1, nz - 1)),
                dma((steps + 1, nz - 1)),
                dma(()),
                dma(()),
                dma((nz - 1,)),
                dma((nz - 1,)),
            ],
            compiler_params=pltpu.CompilerParams(
                collective_id=0, has_side_effects=True, vmem_limit_bytes=60 << 20
            ),
            cost_estimate=pl.CostEstimate(
                flops=2 * rows * width * depth * nz,
                bytes_accessed=4 * rows * cols,
                transcendentals=rows * width,
            ),
        )(query_desc, base_desc, slopes)
        return seq_score, best.reshape(rows)

    return jax.shard_map(
        local,
        mesh=mesh,
        in_specs=(P("qrow", "dbcol"), P("dbcol", "qrow"), P()),
        out_specs=(P("qrow", "dbcol"), P("qrow")),
        check_vma=False,
    )
```

```python
import functools
import math

import jax
import jax.numpy as jnp
from jax import lax
from jax.experimental import pallas as pl
from jax.experimental.pallas import tpu as pltpu
from jax.sharding import PartitionSpec as P

SEQ = 20
WIN = 10
SMAX = 3
NSLOPE = 5

SPREAD_FLOOR = 0.5
SIDE = 64
ABOVE = 24
EARLY = 32
STEP = 128
SUB, LANE = 8, 128
MESH = pl.DeviceIdType.MESH


def rolled(x, by):
    by %= x.shape[1]
    return pltpu.roll(x, by, 1) if by else x


def sheared(x, by, slope):
    if not slope:
        return rolled(x, by)
    width, tiles = x.shape[1], []
    for r in range(0, x.shape[0], SUB):
        tile, shift = x[r : r + SUB, :], (by + slope * r) % width
        if shift % LANE + slope * (SUB - 1) <= LANE:
            tile = pltpu.roll(tile, shift, 1, stride=slope, stride_axis=0)
        else:
            tile = rolled(pltpu.roll(tile, 0, 1, stride=slope, stride_axis=0), shift)
        tiles.append(tile)
    return jnp.concatenate(tiles, 0)


def window_sum(x):
    two = x + rolled(x, -1)
    four = two + rolled(two, -2)
    eight = four + rolled(four, -4)
    return rolled(eight + rolled(two, -8), WIN // 2)


def kernel(
    nq, nz, q_ref, b_ref, slopes_hbm, seq_hbm, best_ref, seq_ref, qs, bs, bt, normed, made, given,
    tops, slopes_ref,
    own_sem, out_sem, side_send, side_recv, base_send, base_recv, pass_send, pass_recv,
    query_send, query_recv, given_send, given_recv, up_send, up_recv, top_send, top_recv,
):
    me_q, me_z = lax.axis_index("qrow"), lax.axis_index("dbcol")
    rows, depth = q_ref.shape
    cols, base_depth = b_ref.shape
    width = cols + 2 * SIDE
    total = cols * nz
    first, last = me_z == 0, me_z == nz - 1

    def remote(src, dst, send, recv, q, z):
        return pltpu.make_async_remote_copy(
            src_ref=src, dst_ref=dst, send_sem=send, recv_sem=recv,
            device_id=(q, z), device_id_type=MESH,
        )

    slot_depth = bs.shape[3]

    inner = jnp.logical_not(first | last)
    beside_first, beside_last = me_z == 1, me_z == nz - 2
    beside = beside_first | beside_last
    end = jnp.where(me_z <= 1, 0, nz - 1)

    def block(k, q, start=0, count=width):
        if slot_depth == base_depth:
            return bs.at[k, q, pl.ds(start, count), :]
        at = pl.multiple_of(q * base_depth, LANE)
        return bs.at[k, 0, pl.ds(start, count), pl.ds(at, base_depth)]

    own = [
        pltpu.make_async_copy(q_ref, qs.at[me_z], own_sem.at[0]),
        pltpu.make_async_copy(b_ref, block(0, me_q, 0, cols), own_sem.at[1]),
        pltpu.make_async_copy(slopes_hbm, slopes_ref, own_sem.at[2]),
    ]
    for copy in own:
        copy.start()

    q_peers = [lax.rem(me_q + d, nq) for d in range(1, nq)]
    z_peers = [lax.rem(me_z + d, nz) for d in range(1, nz)]
    barrier = pltpu.get_barrier_semaphore()
    for z in z_peers:
        pl.semaphore_signal(barrier, inc=1, device_id=(me_q, z), device_id_type=MESH)
    for q in q_peers:
        pl.semaphore_signal(barrier, inc=1, device_id=(q, me_z), device_id_type=MESH)

    @pl.when(me_q == 0)
    def _():
        normed[0:ABOVE, :] = jnp.zeros((ABOVE, width), normed.dtype)

    pl.semaphore_wait(barrier, nq + nz - 2)

    to_left = remote(
        b_ref.at[pl.ds(0, SIDE), :], block(0, me_q, cols, SIDE),
        side_send.at[0], side_recv.at[0], me_q, lax.max(me_z - 1, 0),
    )
    to_right = remote(
        b_ref.at[pl.ds(cols - SIDE, SIDE), :], block(0, me_q, cols + SIDE, SIDE),
        side_send.at[1], side_recv.at[1], me_q, lax.min(me_z + 1, nz - 1),
    )
    from_end = remote(
        b_ref, block(1, me_q, 0, cols), side_send.at[2], side_recv.at[2],
        me_q, jnp.where(first, 1, nz - 2),
    )
    sends_left, sends_right = (me_z >= 2) & (me_z <= nz - 2), (me_z >= 1) & (me_z <= nz - 3)

    @pl.when(sends_left)
    def _():
        to_left.start()

    @pl.when(sends_right)
    def _():
        to_right.start()

    @pl.when(first | last)
    def _():
        from_end.start()

    pieces = [(rows - EARLY, EARLY)]
    pieces += [(r, min(STEP, rows - EARLY - r)) for r in range(0, rows, STEP)]

    def query_copy(p, z):
        start, count = pieces[p]
        return remote(
            q_ref.at[pl.ds(start, count), :], qs.at[me_z, pl.ds(start, count), :],
            query_send.at[p, z - 1], query_recv.at[p, me_z], me_q, z,
        )

    def send_query(p):
        for z in range(1, nz - 1):

            @pl.when(me_z != z)
            def _():
                query_copy(p, z).start()

    def wait_query(p):
        start, count = pieces[p]
        for z in range(nz):

            @pl.when(me_z != z)
            def _():
                remote(
                    q_ref.at[pl.ds(start, count), :], qs.at[z, pl.ds(start, count), :],
                    query_send.at[p, 0], query_recv.at[p, z], me_q, z,
                ).wait_recv()

    for p in range(2):
        send_query(p)

    for copy in own:
        copy.wait()

    @pl.when(sends_right)
    def _():
        to_left.wait_recv()

    @pl.when(sends_left)
    def _():
        to_right.wait_recv()

    @pl.when(beside)
    def _():
        from_end.wait_recv()

    nothing = jnp.zeros((SIDE, base_depth), bs.dtype)

    @pl.when(beside_first)
    def _():
        block(0, me_q, cols + SIDE, SIDE)[...] = block(1, me_q, cols - SIDE, SIDE)[...]
        block(1, me_q, cols, SIDE)[...] = block(0, me_q, 0, SIDE)[...]
        block(1, me_q, cols + SIDE, SIDE)[...] = nothing

    @pl.when(beside_last)
    def _():
        block(0, me_q, cols, SIDE)[...] = block(1, me_q, 0, SIDE)[...]
        block(1, me_q, cols + SIDE, SIDE)[...] = block(0, me_q, cols - SIDE, SIDE)[...]
        block(1, me_q, cols, SIDE)[...] = nothing

    mate = me_q + 1 - 2 * lax.rem(me_q, 2)

    def hand_on(k, q, d):
        return remote(block(k, q), block(k, q), pass_send.at[k, d], pass_recv.at[k, d], mate, me_z)

    def turn(k, q):
        start = pl.multiple_of(q * base_depth, base_depth)
        bt[k, pl.ds(start, base_depth), :] = block(k, q)[...].T

    def base_copy(k, d):
        return remote(
            block(k, me_q), block(k, me_q), base_send.at[k, d - 1], base_recv.at[k, d - 1],
            lax.rem(me_q + 2 * d, nq), me_z,
        )

    sets = [(1, beside), (0, inner)]
    for k, takes in sets:

        @pl.when(takes)
        def _():
            for d in range(1, nq // 2):
                base_copy(k, d).start()
            hand_on(k, me_q, 0).start()

    for p in range(2, len(pieces)):
        send_query(p)

    for k, takes in sets:

        @pl.when(takes)
        def _():
            turn(k, me_q)
            for d in range(1, nq // 2):
                base_copy(k, d).wait_recv()
                q = lax.rem(me_q + nq - 2 * d, nq)
                hand_on(k, q, d).start()
                turn(k, q)

    for k, takes in sets:

        @pl.when(takes)
        def _():
            for d in range(nq // 2):
                q = lax.rem(mate + nq - 2 * d, nq)
                hand_on(k, q, d).wait_recv()
                turn(k, q)

    place = lax.broadcasted_iota(jnp.int32, (1, width), 1)

    def around(z):
        frame = z * cols + jnp.where(place < cols + SIDE, place, place - width)
        reach = jnp.minimum(frame + WIN // 2, total) - jnp.maximum(frame - WIN // 2, 0)
        share = 1.0 / jnp.maximum(reach, 1).astype(jnp.float32)
        return (frame >= 0) & (frame < total), share

    def normalize(k, start, count):
        inside, share = around(end if k else me_z)
        similar = None
        for z in range(nz):
            part = jnp.dot(
                qs[z, start : start + count, :], bt[k, z * depth : (z + 1) * depth, :],
                preferred_element_type=jnp.float32,
            )
            similar = part if similar is None else similar + part
        mean = window_sum(similar) * share
        var = window_sum(similar * similar) * share - mean * mean
        value = (similar - mean) * lax.rsqrt(jnp.maximum(var, SPREAD_FLOOR * SPREAD_FLOOR))
        value = jnp.where(inside, value, 0.0)
        return value.astype(jnp.bfloat16)

    def give(p):
        rows_now = pl.ds(*pieces[p])
        return remote(
            made.at[rows_now, :], given.at[rows_now, :], given_send.at[p], given_recv.at[p],
            me_q, end,
        )

    def normalize_part(p):
        start, count = pieces[p]
        own_rows = pl.ds(ABOVE + start, count)

        @pl.when(inner)
        def _():
            wait_query(p)

        @pl.when(beside)
        def _():
            made[pl.ds(start, count), :] = normalize(1, start, count)
            give(p).start()

        @pl.when(inner)
        def _():
            normed[own_rows, :] = normalize(0, start, count).astype(jnp.float32)

        @pl.when(first | last)
        def _():
            give(p).wait_recv()
            normed[own_rows, :] = given[pl.ds(start, count), :].astype(jnp.float32)

    tried = {}
    for v in range(-SMAX, SMAX + 1):
        used = slopes_ref[0] == v
        for a in range(1, NSLOPE):
            used = used | (slopes_ref[a] == v)
        tried[v] = jnp.where(used, 0.0, -jnp.inf)

    span = ABOVE + STEP
    out_row = lax.broadcasted_iota(jnp.int32, (STEP, span), 0) + ABOVE
    in_row = lax.broadcasted_iota(jnp.int32, (STEP, span), 1)

    def summing(out, into):
        return ((into <= out) & (into > out - SEQ)).astype(jnp.bfloat16)

    band = summing(out_row, in_row)
    band_turned_in = summing(out_row, span - 1 - in_row)
    band_turned_out = summing(span + ABOVE - 1 - out_row, in_row)

    def turning(n, kind):
        row = lax.broadcasted_iota(jnp.int32, (n, n), 0)
        return (row + lax.broadcasted_iota(jnp.int32, (n, n), 1) == n - 1).astype(kind)

    turn_in, turn_out = turning(span, jnp.bfloat16), turning(STEP, jnp.float32)

    written = []

    def score(start):
        block = normed[start : start + span, :]
        exact = block.astype(jnp.bfloat16)
        best = jnp.dot(band, exact, preferred_element_type=jnp.float32)[:, :cols] + tried[0]
        turned = jnp.dot(turn_in, exact, preferred_element_type=jnp.float32)
        down = None
        for v in range(1, SMAX + 1):
            lined = sheared(turned, -v * (span - 1), v).astype(jnp.bfloat16)
            sums = jnp.dot(band_turned_in, lined, preferred_element_type=jnp.float32)
            sums = sheared(sums, v * ABOVE, v)[:, :cols]
            best = jnp.maximum(best, sums + tried[v])
            lined = sheared(block, 0, v).astype(jnp.bfloat16)
            sums = jnp.dot(band_turned_out, lined, preferred_element_type=jnp.float32)
            sums = sheared(sums, -v * (span - 1), v)[:, :cols]
            sums = sums if v == SMAX else sums + tried[-v]
            down = sums if down is None else jnp.maximum(down, sums)
        down = jnp.dot(
            turn_out, down, precision=lax.Precision.HIGHEST, preferred_element_type=jnp.float32
        )
        best = jnp.maximum(best, down)
        best = best * (1.0 / math.sqrt(SEQ))
        done = pl.ds(start, STEP)
        seq_ref[done, :] = best.astype(seq_ref.dtype)
        written.append(
            pltpu.make_async_copy(
                seq_ref.at[done, :], seq_hbm.at[done, :], out_sem.at[start // STEP]
            )
        )
        written[-1].start()
        top = best[:, 0:128]
        for c in range(128, cols, 128):
            top = jnp.maximum(top, best[:, c : c + 128])
        n = start // STEP
        tops[0, n : n + 1, :] = jnp.max(top.T, axis=0, keepdims=True)

    normalize_part(0)
    up = remote(
        normed.at[pl.ds(rows, ABOVE), :], normed.at[pl.ds(0, ABOVE), :],
        up_send, up_recv, lax.min(me_q + 1, nq - 1), me_z,
    )

    @pl.when(me_q < nq - 1)
    def _():
        up.start()

    for p in range(1, len(pieces)):
        normalize_part(p)
        if p == 1:

            @pl.when(me_q > 0)
            def _():
                up.wait_recv()

        score(pieces[p][0])

    peaks = [
        remote(tops.at[0], tops.at[1 + d], top_send.at[d], top_recv.at[d], me_q, z)
        for d, z in enumerate(z_peers)
    ]
    for copy in peaks:
        copy.start()

    @pl.when(sends_left)
    def _():
        to_left.wait_send()

    @pl.when(sends_right)
    def _():
        to_right.wait_send()

    @pl.when(first | last)
    def _():
        from_end.wait_send()

    for k, takes in sets:

        @pl.when(takes)
        def _():
            for d in range(1, nq // 2):
                base_copy(k, d).wait_send()
            for d in range(nq // 2):
                hand_on(k, lax.rem(me_q + nq - 2 * d, nq), d).wait_send()

    for p in range(len(pieces)):

        @pl.when(beside)
        def _():
            give(p).wait_send()

        for z in range(1, nz - 1):

            @pl.when(me_z != z)
            def _():
                query_copy(p, z).wait_send()

    @pl.when(me_q < nq - 1)
    def _():
        up.wait_send()

    for copy in written + peaks:
        copy.wait()
    best = tops[0]
    for d in range(1, nz):
        best = jnp.maximum(best, tops[d])
    best_ref[...] = best


def solution(mesh):
    nq, nz = mesh.shape["qrow"], mesh.shape["dbcol"]

    def local(query_desc, base_desc, slopes):
        rows, depth = query_desc.shape
        cols, base_depth = base_desc.shape
        width = cols + 2 * SIDE
        slots = (nq, width, base_depth) if base_depth % LANE else (1, width, base_depth * nq)
        steps = rows // STEP
        dma = pltpu.SemaphoreType.DMA
        hbm = pl.BlockSpec(memory_space=pltpu.HBM)
        vmem = pl.BlockSpec(memory_space=pltpu.VMEM)
        seq_score, best = pl.pallas_call(
            functools.partial(kernel, nq, nz),
            out_shape=(
                jax.ShapeDtypeStruct((rows, cols), jnp.bfloat16),
                jax.ShapeDtypeStruct((steps, STEP), jnp.float32),
            ),
            in_specs=[hbm, hbm, hbm],
            out_specs=(hbm, vmem),
            scratch_shapes=[
                pltpu.VMEM((rows, cols), jnp.bfloat16),
                pltpu.VMEM((nz, rows, depth), jnp.bfloat16),
                pltpu.VMEM((2, *slots), jnp.bfloat16),
                pltpu.VMEM((2, base_depth * nq, width), jnp.bfloat16),
                pltpu.VMEM((ABOVE + rows, width), jnp.float32),
                pltpu.VMEM((rows, width), jnp.bfloat16),
                pltpu.VMEM((rows, width), jnp.bfloat16),
                pltpu.VMEM((nz, steps, STEP), jnp.float32),
                pltpu.SMEM((NSLOPE,), jnp.int32),
                dma((3,)),
                dma((steps,)),
                dma((3,)),
                dma((3,)),
                dma((2, nq // 2 - 1)),
                dma((2, nq // 2 - 1)),
                dma((2, nq // 2)),
                dma((2, nq // 2)),
                dma((steps + 1, nz - 2)),
                dma((steps + 1, nz)),
                dma((steps + 1,)),
                dma((steps + 1,)),
                dma(()),
                dma(()),
                dma((nz - 1,)),
                dma((nz - 1,)),
            ],
            compiler_params=pltpu.CompilerParams(
                collective_id=0, has_side_effects=True, vmem_limit_bytes=60 << 20
            ),
            cost_estimate=pl.CostEstimate(
                flops=2 * rows * width * depth * nz,
                bytes_accessed=4 * rows * cols,
                transcendentals=rows * width,
            ),
        )(query_desc, base_desc, slopes)
        return seq_score, best.reshape(rows)

    return jax.shard_map(
        local,
        mesh=mesh,
        in_specs=(P("qrow", "dbcol"), P("dbcol", "qrow"), P()),
        out_specs=(P("qrow", "dbcol"), P("qrow")),
        check_vma=False,
    )
```

```python
import functools
import math

import jax
import jax.numpy as jnp
from jax import lax
from jax.experimental import pallas as pl
from jax.experimental.pallas import tpu as pltpu
from jax.sharding import PartitionSpec as P

SEQ = 20
WIN = 10
SMAX = 3
NSLOPE = 5

SPREAD_FLOOR = 0.5
SIDE = 64
ABOVE = 24
EARLY = 32
AHEAD = 3
STEP = 128
SUB, LANE = 8, 128
MESH = pl.DeviceIdType.MESH


def rolled(x, by):
    by %= x.shape[1]
    return pltpu.roll(x, by, 1) if by else x


def sheared(x, by, slope):
    if not slope:
        return rolled(x, by)
    width, tiles = x.shape[1], []
    for r in range(0, x.shape[0], SUB):
        tile, shift = x[r : r + SUB, :], (by + slope * r) % width
        if shift % LANE + slope * (SUB - 1) <= LANE:
            tile = pltpu.roll(tile, shift, 1, stride=slope, stride_axis=0)
        else:
            tile = rolled(pltpu.roll(tile, 0, 1, stride=slope, stride_axis=0), shift)
        tiles.append(tile)
    return jnp.concatenate(tiles, 0)


def window_sum(x):
    two = x + rolled(x, -1)
    four = two + rolled(two, -2)
    eight = four + rolled(four, -4)
    return rolled(eight + rolled(two, -8), WIN // 2)


def kernel(
    nq, nz, q_ref, b_ref, slopes_hbm, seq_hbm, best_ref, seq_ref, qs, bs, bt, normed, tops, slopes_ref,
    own_sem, out_sem, side_send, side_recv, base_send, base_recv, pass_send, pass_recv,
    query_send, query_recv, up_send, up_recv, top_send, top_recv,
):
    me_q, me_z = lax.axis_index("qrow"), lax.axis_index("dbcol")
    rows, depth = q_ref.shape
    cols, base_depth = b_ref.shape
    width = cols + 2 * SIDE
    total = cols * nz
    first, last = me_z == 0, me_z == nz - 1

    def remote(src, dst, send, recv, q, z):
        return pltpu.make_async_remote_copy(
            src_ref=src, dst_ref=dst, send_sem=send, recv_sem=recv,
            device_id=(q, z), device_id_type=MESH,
        )

    slot_depth = bs.shape[2]

    def mine(start, count):
        if slot_depth == base_depth:
            return me_q, pl.ds(start, count), pl.ds(0, base_depth)
        return 0, pl.ds(start, count), pl.ds(pl.multiple_of(me_q * base_depth, LANE), base_depth)

    own = [
        pltpu.make_async_copy(q_ref, qs.at[me_z], own_sem.at[0]),
        pltpu.make_async_copy(b_ref, bs.at[mine(0, cols)], own_sem.at[1]),
        pltpu.make_async_copy(slopes_hbm, slopes_ref, own_sem.at[2]),
    ]
    for copy in own:
        copy.start()

    q_peers = [lax.rem(me_q + d, nq) for d in range(1, nq)]
    z_peers = [lax.rem(me_z + d, nz) for d in range(1, nz)]
    barrier = pltpu.get_barrier_semaphore()
    for z in z_peers:
        pl.semaphore_signal(barrier, inc=1, device_id=(me_q, z), device_id_type=MESH)
    for q in q_peers:
        pl.semaphore_signal(barrier, inc=1, device_id=(q, me_z), device_id_type=MESH)

    @pl.when(last)
    def _():
        bs[mine(cols, SIDE)] = jnp.zeros((SIDE, base_depth), bs.dtype)

    @pl.when(first)
    def _():
        bs[mine(cols + SIDE, SIDE)] = jnp.zeros((SIDE, base_depth), bs.dtype)

    @pl.when(me_q == 0)
    def _():
        normed[0:ABOVE, :] = jnp.zeros((ABOVE, width), normed.dtype)

    pl.semaphore_wait(barrier, nq + nz - 2)

    to_left = remote(
        b_ref.at[pl.ds(0, SIDE), :], bs.at[mine(cols, SIDE)],
        side_send.at[0], side_recv.at[0], me_q, lax.max(me_z - 1, 0),
    )
    to_right = remote(
        b_ref.at[pl.ds(cols - SIDE, SIDE), :], bs.at[mine(cols + SIDE, SIDE)],
        side_send.at[1], side_recv.at[1], me_q, lax.min(me_z + 1, nz - 1),
    )

    @pl.when(jnp.logical_not(first))
    def _():
        to_left.start()

    @pl.when(jnp.logical_not(last))
    def _():
        to_right.start()

    pieces = [(rows - EARLY, EARLY)]
    pieces += [(r, min(STEP, rows - EARLY - r)) for r in range(0, rows, STEP)]

    def send_query(p):
        start, count = pieces[p]
        copies = [
            remote(
                q_ref.at[pl.ds(start, count), :], qs.at[me_z, pl.ds(start, count), :],
                query_send.at[p, d], query_recv.at[p, d], me_q, z,
            )
            for d, z in enumerate(z_peers)
        ]
        for copy in copies:
            copy.start()
        return copies

    query = [send_query(p) for p in range(AHEAD - 1)]

    @pl.when(jnp.logical_not(last))
    def _():
        to_left.wait_recv()

    @pl.when(jnp.logical_not(first))
    def _():
        to_right.wait_recv()

    for copy in own:
        copy.wait()

    def block(q):
        if slot_depth == base_depth:
            return bs.at[q]
        start = pl.multiple_of(q * base_depth, LANE)
        return bs.at[0, :, pl.ds(start, base_depth)]

    def hand_on(q, d):
        copy = remote(block(q), block(q), pass_send.at[d], pass_recv.at[d], mate, me_z)
        copy.start()
        return copy

    def turn(q):
        start = pl.multiple_of(q * base_depth, base_depth)
        bt[pl.ds(start, base_depth), :] = block(q)[...].T

    mate = me_q + 1 - 2 * lax.rem(me_q, 2)
    base = [
        remote(
            block(me_q), block(me_q), base_send.at[d - 1], base_recv.at[d - 1],
            lax.rem(me_q + 2 * d, nq), me_z,
        )
        for d in range(1, nq // 2)
    ]
    for copy in base:
        copy.start()
    handed = [hand_on(me_q, 0)]
    query.append(send_query(AHEAD - 1))
    turn(me_q)
    for d in range(1, nq // 2):
        base[d - 1].wait_recv()
        q = lax.rem(me_q + nq - 2 * d, nq)
        handed.append(hand_on(q, d))
        turn(q)
    for d in range(nq // 2):
        handed[d].wait_recv()
        turn(lax.rem(mate + nq - 2 * d, nq))

    place = lax.broadcasted_iota(jnp.int32, (1, width), 1)
    frame = me_z * cols + jnp.where(place < cols + SIDE, place, place - width)
    inside = (frame >= 0) & (frame < total)
    reach = jnp.minimum(frame + WIN // 2, total) - jnp.maximum(frame - WIN // 2, 0)
    share = 1.0 / jnp.maximum(reach, 1).astype(jnp.float32)

    def normalize(start, count):
        similar = None
        for z in range(nz):
            part = jnp.dot(
                qs[z, start : start + count, :], bt[z * depth : (z + 1) * depth, :],
                preferred_element_type=jnp.float32,
            )
            similar = part if similar is None else similar + part
        mean = window_sum(similar) * share
        var = window_sum(similar * similar) * share - mean * mean
        value = (similar - mean) * lax.rsqrt(jnp.maximum(var, SPREAD_FLOOR * SPREAD_FLOOR))
        value = jnp.where(inside, value, 0.0)
        normed[ABOVE + start : ABOVE + start + count, :] = value.astype(jnp.bfloat16).astype(
            jnp.float32
        )

    tried = {}
    for v in range(-SMAX, SMAX + 1):
        used = slopes_ref[0] == v
        for a in range(1, NSLOPE):
            used = used | (slopes_ref[a] == v)
        tried[v] = jnp.where(used, 0.0, -jnp.inf)

    span = ABOVE + STEP
    out_row = lax.broadcasted_iota(jnp.int32, (STEP, span), 0) + ABOVE
    in_row = lax.broadcasted_iota(jnp.int32, (STEP, span), 1)

    def summing(out, into):
        return ((into <= out) & (into > out - SEQ)).astype(jnp.bfloat16)

    band = summing(out_row, in_row)
    band_turned_in = summing(out_row, span - 1 - in_row)
    band_turned_out = summing(span + ABOVE - 1 - out_row, in_row)

    def turning(n, kind):
        row = lax.broadcasted_iota(jnp.int32, (n, n), 0)
        return (row + lax.broadcasted_iota(jnp.int32, (n, n), 1) == n - 1).astype(kind)

    turn_in, turn_out = turning(span, jnp.bfloat16), turning(STEP, jnp.bfloat16)

    written = []

    def score(start):
        block = normed[start : start + span, :]
        exact = block.astype(jnp.bfloat16)
        best = jnp.dot(band, exact, preferred_element_type=jnp.float32)[:, :cols] + tried[0]
        turned = jnp.dot(turn_in, exact, preferred_element_type=jnp.float32)
        slopes = range(1, SMAX + 1)
        lined = [sheared(turned, -v * (span - 1), v).astype(jnp.bfloat16) for v in slopes]
        ups = jnp.dot(
            band_turned_in, jnp.concatenate(lined, 1), preferred_element_type=jnp.float32
        )
        lined = [sheared(block, 0, v).astype(jnp.bfloat16) for v in slopes]
        downs = jnp.dot(
            band_turned_out, jnp.concatenate(lined, 1), preferred_element_type=jnp.float32
        )
        down = None
        for v in slopes:
            at = (v - 1) * width
            sums = sheared(downs[:, at : at + width], -v * (span - 1), v)[:, :cols]
            sums = sums if v == SMAX else sums + tried[-v]
            down = sums if down is None else jnp.maximum(down, sums)
        high = down.astype(jnp.bfloat16)
        rest = down - high.astype(jnp.float32)
        middle = rest.astype(jnp.bfloat16)
        low = (rest - middle.astype(jnp.float32)).astype(jnp.bfloat16)
        parts = jnp.dot(
            turn_out, jnp.concatenate([high, middle, low], 1), preferred_element_type=jnp.float32
        )
        for v in slopes:
            at = (v - 1) * width
            sums = sheared(ups[:, at : at + width], v * ABOVE, v)[:, :cols]
            best = jnp.maximum(best, sums + tried[v])
        down = parts[:, :cols] + (parts[:, cols : 2 * cols] + parts[:, 2 * cols :])
        best = jnp.maximum(best, down)
        best = best * (1.0 / math.sqrt(SEQ))
        done = pl.ds(start, STEP)
        seq_ref[done, :] = best.astype(seq_ref.dtype)
        written.append(
            pltpu.make_async_copy(
                seq_ref.at[done, :], seq_hbm.at[done, :], out_sem.at[start // STEP]
            )
        )
        written[-1].start()
        top = best[:, 0:128]
        for c in range(128, cols, 128):
            top = jnp.maximum(top, best[:, c : c + 128])
        n = start // STEP
        tops[0, n : n + 1, :] = jnp.max(top.T, axis=0, keepdims=True)

    for copy in query[0]:
        copy.wait_recv()
    normalize(*pieces[0])
    up = remote(
        normed.at[pl.ds(rows, ABOVE), :], normed.at[pl.ds(0, ABOVE), :],
        up_send, up_recv, lax.min(me_q + 1, nq - 1), me_z,
    )

    @pl.when(me_q < nq - 1)
    def _():
        up.start()

    for p in range(1, len(pieces)):
        for copy in query[p]:
            copy.wait_recv()
        if p + AHEAD - 1 < len(pieces):
            for copy in query[p]:
                copy.wait_send()
            query.append(send_query(p + AHEAD - 1))
        normalize(*pieces[p])
        if p == 1:

            @pl.when(me_q > 0)
            def _():
                up.wait_recv()

        score(pieces[p][0])

    peaks = [
        remote(tops.at[0], tops.at[1 + d], top_send.at[d], top_recv.at[d], me_q, z)
        for d, z in enumerate(z_peers)
    ]
    for copy in peaks:
        copy.start()

    @pl.when(jnp.logical_not(first))
    def _():
        to_left.wait_send()

    @pl.when(jnp.logical_not(last))
    def _():
        to_right.wait_send()

    @pl.when(me_q < nq - 1)
    def _():
        up.wait_send()

    for copy in base + handed:
        copy.wait_send()
    for p in [0] + list(range(max(1, len(pieces) - AHEAD + 1), len(pieces))):
        for copy in query[p]:
            copy.wait_send()
    for copy in written + peaks:
        copy.wait()
    best = tops[0]
    for d in range(1, nz):
        best = jnp.maximum(best, tops[d])
    best_ref[...] = best


def solution(mesh):
    nq, nz = mesh.shape["qrow"], mesh.shape["dbcol"]

    def local(query_desc, base_desc, slopes):
        rows, depth = query_desc.shape
        cols, base_depth = base_desc.shape
        width = cols + 2 * SIDE
        slots = (nq, width, base_depth) if base_depth % LANE else (1, width, base_depth * nq)
        steps = rows // STEP
        dma = pltpu.SemaphoreType.DMA
        hbm = pl.BlockSpec(memory_space=pltpu.HBM)
        vmem = pl.BlockSpec(memory_space=pltpu.VMEM)
        seq_score, best = pl.pallas_call(
            functools.partial(kernel, nq, nz),
            out_shape=(
                jax.ShapeDtypeStruct((rows, cols), jnp.bfloat16),
                jax.ShapeDtypeStruct((steps, STEP), jnp.float32),
            ),
            in_specs=[hbm, hbm, hbm],
            out_specs=(hbm, vmem),
            scratch_shapes=[
                pltpu.VMEM((rows, cols), jnp.bfloat16),
                pltpu.VMEM((nz, rows, depth), jnp.bfloat16),
                pltpu.VMEM(slots, jnp.bfloat16),
                pltpu.VMEM((base_depth * nq, width), jnp.bfloat16),
                pltpu.VMEM((ABOVE + rows, width), jnp.float32),
                pltpu.VMEM((nz, steps, STEP), jnp.float32),
                pltpu.SMEM((NSLOPE,), jnp.int32),
                dma((3,)),
                dma((steps,)),
                dma((2,)),
                dma((2,)),
                dma((nq // 2 - 1,)),
                dma((nq // 2 - 1,)),
                dma((nq // 2,)),
                dma((nq // 2,)),
                dma((steps + 1, nz - 1)),
                dma((steps + 1, nz - 1)),
                dma(()),
                dma(()),
                dma((nz - 1,)),
                dma((nz - 1,)),
            ],
            compiler_params=pltpu.CompilerParams(
                collective_id=0, has_side_effects=True, vmem_limit_bytes=60 << 20
            ),
            cost_estimate=pl.CostEstimate(
                flops=2 * rows * width * depth * nz,
                bytes_accessed=4 * rows * cols,
                transcendentals=rows * width,
            ),
        )(query_desc, base_desc, slopes)
        return seq_score, best.reshape(rows)

    return jax.shard_map(
        local,
        mesh=mesh,
        in_specs=(P("qrow", "dbcol"), P("dbcol", "qrow"), P()),
        out_specs=(P("qrow", "dbcol"), P("qrow")),
        check_vma=False,
    )
```

```python
import functools
import math

import jax
import jax.numpy as jnp
from jax import lax
from jax.experimental import pallas as pl
from jax.experimental.pallas import tpu as pltpu
from jax.sharding import PartitionSpec as P

SEQ = 20
WIN = 10
SMAX = 3
NSLOPE = 5

SPREAD_FLOOR = 0.5
SIDE = 64
ABOVE = 24
EARLY = 32
STEP = 128
SUB, LANE = 8, 128
MESH = pl.DeviceIdType.MESH


def rolled(x, by):
    by %= x.shape[1]
    return pltpu.roll(x, by, 1) if by else x


def sheared(x, by, slope):
    if not slope:
        return rolled(x, by)
    width, tiles = x.shape[1], []
    for r in range(0, x.shape[0], SUB):
        tile, shift = x[r : r + SUB, :], (by + slope * r) % width
        if shift % LANE + slope * (SUB - 1) <= LANE:
            tile = pltpu.roll(tile, shift, 1, stride=slope, stride_axis=0)
        else:
            tile = rolled(pltpu.roll(tile, 0, 1, stride=slope, stride_axis=0), shift)
        tiles.append(tile)
    return jnp.concatenate(tiles, 0)


def window_sum(x):
    two = x + rolled(x, -1)
    four = two + rolled(two, -2)
    eight = four + rolled(four, -4)
    return rolled(eight + rolled(two, -8), WIN // 2)


def kernel(
    nq, nz, q_ref, b_ref, slopes_hbm, seq_hbm, best_ref, seq_ref, qs, bs, bt, normed, tops, slopes_ref,
    own_sem, out_sem, side_send, side_recv, base_send, base_recv, pass_send, pass_recv,
    query_send, query_recv, up_send, up_recv, top_send, top_recv,
):
    me_q, me_z = lax.axis_index("qrow"), lax.axis_index("dbcol")
    rows, depth = q_ref.shape
    cols, base_depth = b_ref.shape
    width = cols + 2 * SIDE
    total = cols * nz
    first, last = me_z == 0, me_z == nz - 1

    def remote(src, dst, send, recv, q, z):
        return pltpu.make_async_remote_copy(
            src_ref=src, dst_ref=dst, send_sem=send, recv_sem=recv,
            device_id=(q, z), device_id_type=MESH,
        )

    slot_depth = bs.shape[2]

    def mine(start, count):
        if slot_depth == base_depth:
            return me_q, pl.ds(start, count), pl.ds(0, base_depth)
        return 0, pl.ds(start, count), pl.ds(pl.multiple_of(me_q * base_depth, LANE), base_depth)

    own = [
        pltpu.make_async_copy(q_ref, qs.at[me_z], own_sem.at[0]),
        pltpu.make_async_copy(b_ref, bs.at[mine(0, cols)], own_sem.at[1]),
        pltpu.make_async_copy(slopes_hbm, slopes_ref, own_sem.at[2]),
    ]
    for copy in own:
        copy.start()

    q_peers = [lax.rem(me_q + d, nq) for d in range(1, nq)]
    z_peers = [lax.rem(me_z + d, nz) for d in range(1, nz)]
    barrier = pltpu.get_barrier_semaphore()
    for z in z_peers:
        pl.semaphore_signal(barrier, inc=1, device_id=(me_q, z), device_id_type=MESH)
    for q in q_peers:
        pl.semaphore_signal(barrier, inc=1, device_id=(q, me_z), device_id_type=MESH)

    @pl.when(last)
    def _():
        bs[mine(cols, SIDE)] = jnp.zeros((SIDE, base_depth), bs.dtype)

    @pl.when(first)
    def _():
        bs[mine(cols + SIDE, SIDE)] = jnp.zeros((SIDE, base_depth), bs.dtype)

    @pl.when(me_q == 0)
    def _():
        normed[0:ABOVE, :] = jnp.zeros((ABOVE, width), normed.dtype)

    pl.semaphore_wait(barrier, nq + nz - 2)

    to_left = remote(
        b_ref.at[pl.ds(0, SIDE), :], bs.at[mine(cols, SIDE)],
        side_send.at[0], side_recv.at[0], me_q, lax.max(me_z - 1, 0),
    )
    to_right = remote(
        b_ref.at[pl.ds(cols - SIDE, SIDE), :], bs.at[mine(cols + SIDE, SIDE)],
        side_send.at[1], side_recv.at[1], me_q, lax.min(me_z + 1, nz - 1),
    )

    @pl.when(jnp.logical_not(first))
    def _():
        to_left.start()

    @pl.when(jnp.logical_not(last))
    def _():
        to_right.start()

    pieces = [(rows - EARLY, EARLY)]
    pieces += [(r, STEP) for r in range(0, rows - STEP, STEP)]
    pieces += [(rows - STEP, STEP - 2 * EARLY), (rows - 2 * EARLY, EARLY)]

    def send_query(p):
        start, count = pieces[p]
        copies = [
            remote(
                q_ref.at[pl.ds(start, count), :], qs.at[me_z, pl.ds(start, count), :],
                query_send.at[p, d], query_recv.at[p, d], me_q, z,
            )
            for d, z in enumerate(z_peers)
        ]
        for copy in copies:
            copy.start()
        return copies

    query = [send_query(p) for p in range(2)]

    @pl.when(jnp.logical_not(last))
    def _():
        to_left.wait_recv()

    @pl.when(jnp.logical_not(first))
    def _():
        to_right.wait_recv()

    for copy in own:
        copy.wait()

    def block(q):
        if slot_depth == base_depth:
            return bs.at[q]
        start = pl.multiple_of(q * base_depth, LANE)
        return bs.at[0, :, pl.ds(start, base_depth)]

    def hand_on(q, d):
        copy = remote(block(q), block(q), pass_send.at[d], pass_recv.at[d], mate, me_z)
        copy.start()
        return copy

    def turn(q):
        start = pl.multiple_of(q * base_depth, base_depth)
        bt[pl.ds(start, base_depth), :] = block(q)[...].T

    mate = me_q + 1 - 2 * lax.rem(me_q, 2)
    base = [
        remote(
            block(me_q), block(me_q), base_send.at[d - 1], base_recv.at[d - 1],
            lax.rem(me_q + 2 * d, nq), me_z,
        )
        for d in range(1, nq // 2)
    ]
    for copy in base:
        copy.start()
    handed = [hand_on(me_q, 0)]
    query += [send_query(p) for p in range(2, len(pieces))]
    turn(me_q)
    for d in range(1, nq // 2):
        base[d - 1].wait_recv()
        q = lax.rem(me_q + nq - 2 * d, nq)
        handed.append(hand_on(q, d))
        turn(q)
    for d in range(nq // 2):
        handed[d].wait_recv()
        turn(lax.rem(mate + nq - 2 * d, nq))

    place = lax.broadcasted_iota(jnp.int32, (1, width), 1)
    frame = me_z * cols + jnp.where(place < cols + SIDE, place, place - width)
    inside = (frame >= 0) & (frame < total)
    reach = jnp.minimum(frame + WIN // 2, total) - jnp.maximum(frame - WIN // 2, 0)
    share = 1.0 / jnp.maximum(reach, 1).astype(jnp.float32)

    def normalize(start, count):
        similar = None
        for z in range(nz):
            part = jnp.dot(
                qs[z, start : start + count, :], bt[z * depth : (z + 1) * depth, :],
                preferred_element_type=jnp.float32,
            )
            similar = part if similar is None else similar + part
        mean = window_sum(similar) * share
        var = window_sum(similar * similar) * share - mean * mean
        value = (similar - mean) * lax.rsqrt(jnp.maximum(var, SPREAD_FLOOR * SPREAD_FLOOR))
        value = jnp.where(inside, value, 0.0)
        normed[ABOVE + start : ABOVE + start + count, :] = value.astype(jnp.bfloat16).astype(
            jnp.float32
        )

    tried = {}
    for v in range(-SMAX, SMAX + 1):
        used = slopes_ref[0] == v
        for a in range(1, NSLOPE):
            used = used | (slopes_ref[a] == v)
        tried[v] = jnp.where(used, 0.0, -jnp.inf)

    span = ABOVE + STEP
    out_row = lax.broadcasted_iota(jnp.int32, (STEP, span), 0) + ABOVE
    in_row = lax.broadcasted_iota(jnp.int32, (STEP, span), 1)

    def summing(out, into):
        return ((into <= out) & (into > out - SEQ)).astype(jnp.bfloat16)

    band = summing(out_row, in_row)
    band_turned_in = summing(out_row, span - 1 - in_row)
    band_turned_out = summing(span + ABOVE - 1 - out_row, in_row)

    def turning(n, kind):
        row = lax.broadcasted_iota(jnp.int32, (n, n), 0)
        return (row + lax.broadcasted_iota(jnp.int32, (n, n), 1) == n - 1).astype(kind)

    turn_in, turn_out = turning(span, jnp.bfloat16), turning(STEP, jnp.bfloat16)

    written = []

    def score(start):
        block = normed[start : start + span, :]
        exact = block.astype(jnp.bfloat16)
        best = jnp.dot(band, exact, preferred_element_type=jnp.float32)[:, :cols] + tried[0]
        turned = jnp.dot(turn_in, exact, preferred_element_type=jnp.float32)
        slopes = range(1, SMAX + 1)
        lined = [sheared(turned, -v * (span - 1), v).astype(jnp.bfloat16) for v in slopes]
        ups = jnp.dot(
            band_turned_in, jnp.concatenate(lined, 1), preferred_element_type=jnp.float32
        )
        lined = [sheared(block, 0, v).astype(jnp.bfloat16) for v in slopes]
        downs = jnp.dot(
            band_turned_out, jnp.concatenate(lined, 1), preferred_element_type=jnp.float32
        )
        down = None
        for v in slopes:
            at = (v - 1) * width
            sums = sheared(downs[:, at : at + width], -v * (span - 1), v)[:, :cols]
            sums = sums if v == SMAX else sums + tried[-v]
            down = sums if down is None else jnp.maximum(down, sums)
        high = down.astype(jnp.bfloat16)
        rest = down - high.astype(jnp.float32)
        middle = rest.astype(jnp.bfloat16)
        low = (rest - middle.astype(jnp.float32)).astype(jnp.bfloat16)
        parts = jnp.dot(
            turn_out, jnp.concatenate([high, middle, low], 1), preferred_element_type=jnp.float32
        )
        for v in slopes:
            at = (v - 1) * width
            sums = sheared(ups[:, at : at + width], v * ABOVE, v)[:, :cols]
            best = jnp.maximum(best, sums + tried[v])
        down = parts[:, :cols] + (parts[:, cols : 2 * cols] + parts[:, 2 * cols :])
        best = jnp.maximum(best, down)
        best = best * (1.0 / math.sqrt(SEQ))
        done = pl.ds(start, STEP)
        seq_ref[done, :] = best.astype(seq_ref.dtype)
        written.append(
            pltpu.make_async_copy(
                seq_ref.at[done, :], seq_hbm.at[done, :], out_sem.at[start // STEP]
            )
        )
        written[-1].start()
        top = best[:, 0:128]
        for c in range(128, cols, 128):
            top = jnp.maximum(top, best[:, c : c + 128])
        n = start // STEP
        tops[0, n : n + 1, :] = jnp.max(top.T, axis=0, keepdims=True)

    for copy in query[0]:
        copy.wait_recv()
    normalize(*pieces[0])
    up = remote(
        normed.at[pl.ds(rows, ABOVE), :], normed.at[pl.ds(0, ABOVE), :],
        up_send, up_recv, lax.min(me_q + 1, nq - 1), me_z,
    )

    @pl.when(me_q < nq - 1)
    def _():
        up.start()

    for p in range(1, len(pieces)):
        for copy in query[p]:
            copy.wait_recv()
        normalize(*pieces[p])
        if p == 1:

            @pl.when(me_q > 0)
            def _():
                up.wait_recv()

        if p < len(pieces) - 2:
            score(pieces[p][0])
    score(rows - STEP)

    peaks = [
        remote(tops.at[0], tops.at[1 + d], top_send.at[d], top_recv.at[d], me_q, z)
        for d, z in enumerate(z_peers)
    ]
    for copy in peaks:
        copy.start()

    @pl.when(jnp.logical_not(first))
    def _():
        to_left.wait_send()

    @pl.when(jnp.logical_not(last))
    def _():
        to_right.wait_send()

    @pl.when(me_q < nq - 1)
    def _():
        up.wait_send()

    for copy in base + handed:
        copy.wait_send()
    for copies in query:
        for copy in copies:
            copy.wait_send()
    for copy in written + peaks:
        copy.wait()
    best = tops[0]
    for d in range(1, nz):
        best = jnp.maximum(best, tops[d])
    best_ref[...] = best


def solution(mesh):
    nq, nz = mesh.shape["qrow"], mesh.shape["dbcol"]

    def local(query_desc, base_desc, slopes):
        rows, depth = query_desc.shape
        cols, base_depth = base_desc.shape
        width = cols + 2 * SIDE
        slots = (nq, width, base_depth) if base_depth % LANE else (1, width, base_depth * nq)
        steps = rows // STEP
        dma = pltpu.SemaphoreType.DMA
        hbm = pl.BlockSpec(memory_space=pltpu.HBM)
        vmem = pl.BlockSpec(memory_space=pltpu.VMEM)
        seq_score, best = pl.pallas_call(
            functools.partial(kernel, nq, nz),
            out_shape=(
                jax.ShapeDtypeStruct((rows, cols), jnp.bfloat16),
                jax.ShapeDtypeStruct((steps, STEP), jnp.float32),
            ),
            in_specs=[hbm, hbm, hbm],
            out_specs=(hbm, vmem),
            scratch_shapes=[
                pltpu.VMEM((rows, cols), jnp.bfloat16),
                pltpu.VMEM((nz, rows, depth), jnp.bfloat16),
                pltpu.VMEM(slots, jnp.bfloat16),
                pltpu.VMEM((base_depth * nq, width), jnp.bfloat16),
                pltpu.VMEM((ABOVE + rows, width), jnp.float32),
                pltpu.VMEM((nz, steps, STEP), jnp.float32),
                pltpu.SMEM((NSLOPE,), jnp.int32),
                dma((3,)),
                dma((steps,)),
                dma((2,)),
                dma((2,)),
                dma((nq // 2 - 1,)),
                dma((nq // 2 - 1,)),
                dma((nq // 2,)),
                dma((nq // 2,)),
                dma((steps + 2, nz - 1)),
                dma((steps + 2, nz - 1)),
                dma(()),
                dma(()),
                dma((nz - 1,)),
                dma((nz - 1,)),
            ],
            compiler_params=pltpu.CompilerParams(
                collective_id=0, has_side_effects=True, vmem_limit_bytes=60 << 20
            ),
            cost_estimate=pl.CostEstimate(
                flops=2 * rows * width * depth * nz,
                bytes_accessed=4 * rows * cols,
                transcendentals=rows * width,
            ),
        )(query_desc, base_desc, slopes)
        return seq_score, best.reshape(rows)

    return jax.shard_map(
        local,
        mesh=mesh,
        in_specs=(P("qrow", "dbcol"), P("dbcol", "qrow"), P()),
        out_specs=(P("qrow", "dbcol"), P("qrow")),
        check_vma=False,
    )
```
